1024 devices in a mesh: outer: 4 (over x), inner: 256 (over y, z, core).
Axes of the slice: x: 4, y: 4, z: 32, core: 2. Of those that a mesh axis runs over, the one named last changes fastest.
Arguments:
- image_emb: float32 [8192, 1152], P(('outer', 'inner')), may hold values from -0.27 to 0.27
- text_emb: float32 [8192, 1152], P(('outer', 'inner')), may hold values from -0.27 to 0.27
- labels: int32 [8192], replicated, may hold values from 0 to 8191, each once
- scale_logarithm: float32 [1], replicated, may hold values from 1 to 2
- bias: float32 [1], replicated, may hold values from -2 to -0.5
Outputs:
- image_grad: float32 [8192, 1152], P(('outer', 'inner'))
- text_grad: float32 [8192, 1152], P(('outer', 'inner'))
The draws below stay inside these ranges and needn't reach their ends.
Inputs may be any that keep to these rules, and one draw needn't show every extreme that they name: `labels`: every text index is named by exactly one image.
All inputs are finite; a program needn't handle non-finite values.
Results may differ from the reference program's by a relative error of at most 0.0028.
Values may be sent and summed in bfloat16 or wider, within the bound.
A program may use at most 64 MiB of HBM per device.

```python
import jax
import jax.numpy as jnp
from jax import lax

D = 1152
ROWS_DEV = 8
PAIRS = 8192
N_INNER = 256


def shared_directions(key):
    return jnp.clip(jax.random.normal(key, (32, D), jnp.float32), -4.0, 4.0)


def compose_rows(key, directions, noise, row_scale):
    which_key, sign_key, coef_key = jax.random.split(key, 3)
    which = jax.random.randint(which_key, (PAIRS,), 0, 32)
    signs = (jax.random.randint(sign_key, (PAIRS, 1), 0, 2) * 2 - 1).astype(jnp.float32)
    coefs = jax.random.uniform(coef_key, (PAIRS, 1), jnp.float32, 0.6, 1.2)
    picked = jnp.take(directions, which, axis=0)
    return 0.03 * row_scale * (noise + signs * coefs * picked)


def draw_image_emb(key, part):
    directions = shared_directions(key)
    key = jax.random.fold_in(key, 11)
    noise_key = jax.random.fold_in(key, 0)
    rest_key = jax.random.fold_in(key, 2)
    noise = jnp.clip(jax.random.normal(noise_key, (PAIRS, D), jnp.float32), -4.0, 4.0)
    row_scale = jnp.ones((PAIRS, 1), jnp.float32)
    return compose_rows(rest_key, directions, noise, row_scale)


def draw_text_emb(key, part):
    directions = shared_directions(key)
    key = jax.random.fold_in(key, 23)
    noise_key = jax.random.fold_in(key, 0)
    rest_key = jax.random.fold_in(key, 2)
    noise = jnp.clip(jax.random.normal(noise_key, (PAIRS, D), jnp.float32), -4.0, 4.0)
    row_scale = jnp.ones((PAIRS, 1), jnp.float32)
    return compose_rows(rest_key, directions, noise, row_scale)


def setup_inputs(seed: int = 0) -> dict:
    splits = jax.random.split(jax.random.key(seed), 6)
    image_emb = draw_image_emb(jax.random.fold_in(splits[5], 71), 0)
    text_emb = draw_text_emb(jax.random.fold_in(splits[5], 71), 0)
    labels = jax.random.permutation(splits[2], PAIRS).astype(jnp.int32)
    scale_logarithm = jnp.clip(jax.random.uniform(splits[3], (1,), jnp.float32, 1.0, 2.0), 1.0, 2.0)
    bias = jnp.clip(jax.random.uniform(splits[4], (1,), jnp.float32, -2.0, -0.5), -2.0, -0.5)
    return {"image_emb": image_emb, "text_emb": text_emb, "labels": labels, "scale_logarithm": scale_logarithm, "bias": bias}


epsilon = 1e-06

def normalize(values):
    length = jnp.sqrt(lax.optimization_barrier(jnp.sum(values * values, axis=1, keepdims=True)) + epsilon)
    return (values / length, length)

def unit_back(unit_rows, length, unit_grad):
    return (unit_grad - unit_rows * lax.optimization_barrier(jnp.sum(unit_rows * unit_grad, axis=1, keepdims=True))) / length

def reference(image_emb, text_emb, labels, scale_logarithm, bias):
    image_unit, image_len = normalize(image_emb)
    text_unit, text_len = normalize(text_emb)
    image_low = image_unit.astype(jnp.bfloat16)
    text_reduced_precision = text_unit.astype(jnp.bfloat16)
    logit_scale_factor = jnp.exp(scale_logarithm[0])
    logit_bias_value = bias[0]
    pair_count, feature_count = image_emb.shape
    columns = jnp.arange(pair_count, dtype=jnp.int32)
    label_ints = labels.astype(jnp.int32)
    block_rows = ROWS_DEV * N_INNER
    block_count = pair_count // block_rows

    def block_step(loop_state, index):
        first = (index * block_rows).astype(jnp.int32)
        batch_row_count = lax.dynamic_slice_in_dim(image_low, first, block_rows, 0)
        label_rows = lax.dynamic_slice_in_dim(label_ints, first, block_rows, 0)
        pair_similarity = jnp.dot(batch_row_count, text_reduced_precision.T, preferred_element_type=jnp.float32)
        pair_logit_matrix = logit_scale_factor * pair_similarity + logit_bias_value
        target = jnp.where(label_rows[:, None] == columns[None, :], jnp.float32(1.0), jnp.float32(-1.0))
        weights = -target * jax.nn.sigmoid(-target * pair_logit_matrix)
        weight_reduced_precision = weights.astype(jnp.bfloat16)
        gradient_row_block = logit_scale_factor * jnp.dot(weight_reduced_precision, text_reduced_precision, preferred_element_type=jnp.float32)
        text_gradient_total = loop_state + logit_scale_factor * jnp.dot(weight_reduced_precision.T, batch_row_count, preferred_element_type=jnp.float32)
        return (text_gradient_total, gradient_row_block)
    start = jnp.zeros((pair_count, feature_count), jnp.float32)
    text_unit_grad, grad_blocks = lax.scan(block_step, start, jnp.arange(block_count, dtype=jnp.int32))
    image_unit_grad = grad_blocks.reshape(pair_count, feature_count)
    image_grad = unit_back(image_unit, image_len, image_unit_grad)
    text_grad = unit_back(text_unit, text_len, text_unit_grad)
    return (image_grad, text_grad)
```

```python
import functools

import jax
import jax.numpy as jnp
from jax import lax
from jax.experimental import pallas as pl
from jax.experimental.pallas import tpu as pltpu
from jax.sharding import PartitionSpec as P

EPSILON = 1e-06
X, Y, Z = 4, 4, 32
TEXT_STEPS = (0, 1, -1, 2, -2, 3, -3, 4)
IMAGE_STEPS = (4, -4, 12, -12)
STAGE = 5
BF = jnp.bfloat16
F32 = jnp.float32


def kernel(
    labels_ref, scale_ref, bias_ref, image_ref, text_ref,
    image_out, text_out,
    own_image, tbuf, ibuf, tsend, isend, town, iown, tback, iback,
    tsum, isum, tlast, ilast,
    zt_s, zt_r, zi_s, zi_r, pt_s, pt_r, pi_s, pi_r,
    rt_s, rt_r, ri_s, ri_r, lt_s, lt_r, li_s, li_r,
):
    nk, no = len(TEXT_STEPS), len(IMAGE_STEPS)
    nq = 2 * Y
    rows, width = image_ref.shape
    x = lax.axis_index("outer")
    inner = lax.axis_index("inner")
    core = lax.rem(inner, 2)
    z = lax.rem(inner // 2, Z)
    y = inner // (2 * Z)
    side = 1 - 2 * core

    def device(dx=0, dy=0, dz=0, dc=0):
        place_y = lax.rem(y + dy + Y, Y)
        place_z = lax.rem(z + dz + Z, Z)
        place_c = lax.rem(core + dc, 2)
        return (lax.rem(x + dx + X, X), (place_y * Z + place_z) * 2 + place_c)

    def send(src, dst, send_sem, recv_sem, place):
        pltpu.make_async_remote_copy(
            src_ref=src, dst_ref=dst, send_sem=send_sem, recv_sem=recv_sem,
            device_id=place, device_id_type=pl.DeviceIdType.MESH,
        ).start()

    def wait(ref, sem):
        pltpu.make_async_copy(ref, ref, sem).wait()

    barrier = pltpu.get_barrier_semaphore()
    near = {abs(s) for s in TEXT_STEPS + IMAGE_STEPS if s}
    partners = [device(dz=d) for a in sorted(near, reverse=True) for d in {a % Z, -a % Z}]
    partners += [device(dx=j) for j in range(1, X)]
    partners += [device(dy=q // 2, dc=q % 2) for q in range(1, nq)]
    for place in partners:
        pl.semaphore_signal(barrier, inc=1, device_id=place, device_id_type=pl.DeviceIdType.MESH)

    def normalize(values):
        length = jnp.sqrt(jnp.sum(values * values, axis=1, keepdims=True) + EPSILON)
        return values / length, length

    image_unit, image_len = normalize(image_ref[...])
    text_unit, text_len = normalize(text_ref[...])
    own_image[...] = image_unit.astype(BF)
    tbuf[0, 0] = text_unit.astype(BF)
    scale = jnp.exp(jnp.full((1, 1), scale_ref[0], F32))

    pl.semaphore_wait(barrier, len(partners))

    if STAGE >= 1:
        work = [("i", o, s) for o, s in enumerate(IMAGE_STEPS)]
        work += [("t", k, s) for k, s in enumerate(TEXT_STEPS) if s]
        for what, slot, step in sorted(work, key=lambda w: -abs(w[2])):
            if what == "i":
                send(own_image, ibuf.at[0, slot], zi_s, zi_r.at[slot], device(dz=step))
            else:
                send(tbuf.at[0, 0], tbuf.at[0, slot], zt_s, zt_r.at[slot], device(dz=side * step))

    def spread_text(k):
        if k:
            wait(tbuf.at[0, k], zt_r.at[k])
        if STAGE >= 2:
            for j in range(1, X):
                send(tbuf.at[0, k], tbuf.at[j, k], pt_s, pt_r, device(dx=j))

    def spread_image(o):
        wait(ibuf.at[0, o], zi_r.at[o])
        if STAGE >= 2:
            for q in range(1, nq):
                send(ibuf.at[0, o], ibuf.at[q, o], pi_s, pi_r, device(dy=q // 2, dc=q % 2))

    if STAGE >= 1:
        work = [(abs(s), 0, k) for k, s in enumerate(TEXT_STEPS)]
        work += [(abs(s), 1, o) for o, s in enumerate(IMAGE_STEPS)]
        for _, what, slot in sorted(work):
            (spread_image if what else spread_text)(slot)

    if STAGE >= 2:
        wait(tbuf.at[1:], pt_r)
        wait(ibuf.at[1:], pi_r)

    if STAGE >= 3:
        texts = tbuf[...].astype(F32).reshape(X * nk * rows, width).astype(BF)
        images = ibuf[...].astype(F32).reshape(nq * no * rows, width).astype(BF)
        similarity = lax.dot_general(
            images, texts, (((1,), (1,)), ((), ())), preferred_element_type=F32
        )
        logits = scale * similarity + bias_ref[0]

        lane = lax.broadcasted_iota(jnp.int32, (rows, 128), 1)
        row = lax.broadcasted_iota(jnp.int32, (rows, 128), 0)
        pieces = []
        for q in range(nq):
            from_y = lax.rem(y - q // 2 + Y, Y)
            from_c = lax.rem(core + q % 2, 2)
            for step in IMAGE_STEPS:
                from_z = lax.rem(z - step + Z, Z)
                first = ((x * Y + from_y) * Z + from_z) * (2 * rows) + from_c * rows
                line = labels_ref[pl.ds(first // 128, 1), :]
                pick = lane == row + lax.rem(first, 128)
                pieces.append(jnp.where(pick, jnp.broadcast_to(line, (rows, 128)), 0))
        label = jnp.sum(jnp.concatenate(pieces, axis=0).astype(F32), axis=1, keepdims=True)

        spot = lax.broadcasted_iota(jnp.int32, (1, X * nk * rows), 1)
        at_row, at_k, at_j = spot % rows, (spot // rows) % nk, spot // (rows * nk)
        step_of = jnp.zeros_like(spot)
        for k, step in enumerate(TEXT_STEPS):
            step_of = jnp.where(at_k == k, step, step_of)
        from_x = lax.rem(x - at_j + X, X)
        from_z = lax.rem(z - side * step_of + Z, Z)
        column = (((from_x * Y + y) * Z + from_z) * 2 + core) * rows + at_row
        match = label == column.astype(F32)

        signed = jnp.where(match, -logits, logits)
        sigmoid = 1.0 / (1.0 + jnp.exp(-signed))
        weights = jnp.where(match, -sigmoid, sigmoid).astype(BF)

        grad = jnp.dot(weights, texts, preferred_element_type=F32)
        grad = grad.reshape(nq, no, rows, width)
        iown[...] = grad[0]
        isend[...] = grad[1:].astype(BF)
    if STAGE >= 4:
        for o in reversed(range(no)):
            for q in range(1, nq):
                send(isend.at[q - 1, o], iback.at[o, q - 1], ri_s, ri_r.at[o],
                     device(dy=-(q // 2), dc=q % 2))
    if STAGE >= 3:
        grad = lax.dot_general(
            weights, images, (((0,), (0,)), ((), ())), preferred_element_type=F32
        )
        grad = grad.reshape(X, nk, rows, width)
        town[...] = grad[0]
        tsend[...] = grad[1:].astype(BF)
    if STAGE >= 4:
        for k in reversed(range(nk)):
            for j in range(1, X):
                send(tsend.at[j - 1, k], tback.at[k, j - 1], rt_s, rt_r.at[k], device(dx=-j))

        def join_image(o):
            wait(iback.at[o], ri_r.at[o])
            total = iown[o] + jnp.sum(iback[o].astype(F32), axis=0)
            isum[o] = total.astype(BF)
            if STAGE >= 5:
                send(isum.at[o], ilast.at[o], li_s, li_r.at[o], device(dz=-IMAGE_STEPS[o]))

        def join_text(k):
            wait(tback.at[k], rt_r.at[k])
            total = town[k] + jnp.sum(tback[k].astype(F32), axis=0)
            if k == 0:
                town[0] = total
            else:
                tsum[k - 1] = total.astype(BF)
                if STAGE >= 5:
                    send(tsum.at[k - 1], tlast.at[k - 1], lt_s, lt_r.at[k - 1],
                         device(dz=-side * TEXT_STEPS[k]))

        for o in reversed(range(no)):
            join_image(o)
        for k in reversed(range(nk)):
            join_text(k)

    def unit_back(unit, length, unit_grad):
        return (unit_grad - unit * jnp.sum(unit * unit_grad, axis=1, keepdims=True)) / length

    if STAGE >= 5:
        for o in range(no):
            wait(ilast.at[o], li_r.at[o])
        image_unit_grad = scale * jnp.sum(ilast[...].astype(F32), axis=0)
        image_out[...] = unit_back(image_unit, image_len, image_unit_grad)
        for k in range(nk - 1):
            wait(tlast.at[k], lt_r.at[k])
        text_unit_grad = scale * (town[0] + jnp.sum(tlast[...].astype(F32), axis=0))
        text_out[...] = unit_back(text_unit, text_len, text_unit_grad)
    else:
        image_out[...] = image_unit
        text_out[...] = text_unit

    if STAGE >= 1:
        wait(ibuf.at[0], zi_s)
        wait(tbuf.at[0, 1:], zt_s)
    if STAGE >= 2:
        wait(tbuf.at[1:], pt_s)
        wait(ibuf.at[1:], pi_s)
    if STAGE >= 4:
        wait(isend, ri_s)
        wait(tsend, rt_s)
    if STAGE >= 5:
        wait(isum, li_s)
        wait(tsum, lt_s)


def per_device(image_emb, text_emb, labels, scale_logarithm, bias):
    rows, width = image_emb.shape
    nk, no, nq = len(TEXT_STEPS), len(IMAGE_STEPS), 2 * Y
    block = (rows, width)
    vmem = pl.BlockSpec(memory_space=pltpu.VMEM)
    smem = pl.BlockSpec(memory_space=pltpu.SMEM)
    one = pltpu.SemaphoreType.DMA
    some = lambda n: pltpu.SemaphoreType.DMA((n,))
    return pl.pallas_call(
        kernel,
        out_shape=[jax.ShapeDtypeStruct(block, F32)] * 2,
        in_specs=[vmem, smem, smem, vmem, vmem],
        out_specs=[vmem, vmem],
        scratch_shapes=[
            pltpu.VMEM(block, BF),
            pltpu.VMEM((X, nk) + block, BF),
            pltpu.VMEM((nq, no) + block, BF),
            pltpu.VMEM((X - 1, nk) + block, BF),
            pltpu.VMEM((nq - 1, no) + block, BF),
            pltpu.VMEM((nk,) + block, F32),
            pltpu.VMEM((no,) + block, F32),
            pltpu.VMEM((nk, X - 1) + block, BF),
            pltpu.VMEM((no, nq - 1) + block, BF),
            pltpu.VMEM((nk - 1,) + block, BF),
            pltpu.VMEM((no,) + block, BF),
            pltpu.VMEM((nk - 1,) + block, BF),
            pltpu.VMEM((no,) + block, BF),
            one, some(nk), one, some(no),
            one, one, one, one,
            one, some(nk), one, some(no),
            one, some(nk - 1), one, some(no),
        ],
        compiler_params=pltpu.CompilerParams(
            collective_id=0, has_side_effects=True, vmem_limit_bytes=48 * 2**20
        ),
    )(labels.reshape(-1, 128), scale_logarithm, bias, image_emb, text_emb)


def solution(mesh):
    rows = P(("outer", "inner"), None)
    return jax.shard_map(
        per_device,
        mesh=mesh,
        in_specs=(rows, rows, P(), P(), P()),
        out_specs=(rows, rows),
        check_vma=False,
    )
```

```python
import functools

import jax
import jax.numpy as jnp
from jax import lax
from jax.experimental import pallas as pl
from jax.experimental.pallas import tpu as pltpu
from jax.sharding import PartitionSpec as P

EPSILON = 1e-06
X, Y, Z = 4, 4, 32
STRIDE = 4
TEXT_STEPS = (4, 3, 2, 1, 0, -1, -2, -3)
IMAGE_STEPS = (12, 4, -4, -12)
STAGE = 5
BF = jnp.bfloat16
F32 = jnp.float32


def kernel(
    labels_hbm, scale_hbm, bias_hbm, image_hbm, text_hbm,
    image_out, text_out,
    own_image, tbuf, ibuf, tsend, isend, town, iown, tback, iback,
    tsum, isum, tlast, ilast,
    zt_s, zt_r, zi_s, zi_r, pt_s, pt_r, pi_s, pi_r,
    rt_s, rt_r, ri_s, ri_r, lt_s, lt_r, li_s, li_r,
    image_ref, text_ref, labels_ref, scale_ref, bias_ref, load, relay, relay_r,
):
    nk, no = len(TEXT_STEPS), len(IMAGE_STEPS)
    nq = 2 * Y
    home = TEXT_STEPS.index(0)
    rows, width = image_ref.shape
    loads = [
        pltpu.make_async_copy(src, dst, load.at[n])
        for n, (src, dst) in enumerate(
            ((image_hbm, image_ref), (text_hbm, text_ref), (labels_hbm, labels_ref),
             (scale_hbm, scale_ref), (bias_hbm, bias_ref))
        )
    ]
    for copy in loads:
        copy.start()
    x = lax.axis_index("outer")
    inner = lax.axis_index("inner")
    core = lax.rem(inner, 2)
    z = lax.rem(inner // 2, Z)
    y = inner // (2 * Z)
    side = 1 - 2 * core

    def device(dx=0, dy=0, dz=0, dc=0):
        place_y = lax.rem(y + dy + Y, Y)
        place_z = lax.rem(z + dz + Z, Z)
        place_c = lax.rem(core + dc, 2)
        return (lax.rem(x + dx + X, X), (place_y * Z + place_z) * 2 + place_c)

    def send(src, dst, send_sem, recv_sem, place):
        pltpu.make_async_remote_copy(
            src_ref=src, dst_ref=dst, send_sem=send_sem, recv_sem=recv_sem,
            device_id=place, device_id_type=pl.DeviceIdType.MESH,
        ).start()

    def wait(ref, sem):
        pltpu.make_async_copy(ref, ref, sem).wait()

    barrier = pltpu.get_barrier_semaphore()
    near = {abs(s) for s in TEXT_STEPS if s}
    partners = [device(dz=d) for a in sorted(near, reverse=True) for d in {a % Z, -a % Z}]
    partners += [device(dx=j) for j in range(1, X)]
    partners += [device(dy=q // 2, dc=q % 2) for q in range(1, nq)]
    for place in partners:
        pl.semaphore_signal(barrier, inc=1, device_id=place, device_id_type=pl.DeviceIdType.MESH)

    def normalize(values):
        length = jnp.sqrt(jnp.sum(values * values, axis=1, keepdims=True) + EPSILON)
        return values / length, length

    for copy in loads:
        copy.wait()
    image_unit, image_len = normalize(image_ref[...])
    text_unit, text_len = normalize(text_ref[...])
    own_image[...] = image_unit.astype(BF)
    tbuf[0, home] = text_unit.astype(BF)
    scale = jnp.exp(jnp.full((1, 1), scale_ref[0], F32))

    pl.semaphore_wait(barrier, len(partners))

    def spread_text(k):
        if STAGE >= 2:
            for j in range(1, X):
                send(tbuf.at[0, k], tbuf.at[j, k], pt_s, pt_r, device(dx=j))

    def spread_image(o):
        if STAGE >= 2:
            for q in range(1, nq):
                send(ibuf.at[0, o], ibuf.at[q, o], pi_s, pi_r, device(dy=q // 2, dc=q % 2))

    if STAGE >= 1:
        for o, step in ((1, STRIDE), (2, -STRIDE)):
            send(own_image, ibuf.at[0, o], zi_s, zi_r.at[o], device(dz=step))
        for k, step in sorted(enumerate(TEXT_STEPS), key=lambda w: abs(w[1])):
            if step:
                send(tbuf.at[0, home], tbuf.at[0, k], zt_s, zt_r.at[k], device(dz=side * step))
        spread_text(home)

        def pull_text(k):
            wait(tbuf.at[0, k], zt_r.at[k])
            spread_text(k)

        for k, step in enumerate(TEXT_STEPS):
            if 0 < abs(step) <= STRIDE // 2:
                pull_text(k)
        for o, step in ((1, STRIDE), (2, -STRIDE)):
            wait(ibuf.at[0, o], zi_r.at[o])
            send(ibuf.at[0, o], relay.at[o - 1], zi_s, relay_r.at[o - 1], device(dz=step))
        for o in (1, 2):
            spread_image(o)
        for k, step in enumerate(TEXT_STEPS):
            if STRIDE // 2 < abs(step):
                pull_text(k)
        for o, step in ((1, STRIDE), (2, -STRIDE)):
            wait(relay.at[o - 1], relay_r.at[o - 1])
            far = 0 if o == 1 else 3
            send(relay.at[o - 1], ibuf.at[0, far], zi_s, zi_r.at[far], device(dz=step))
        for o in (0, 3):
            wait(ibuf.at[0, o], zi_r.at[o])
            spread_image(o)

    if STAGE >= 2:
        wait(tbuf.at[1:], pt_r)
        wait(ibuf.at[1:], pi_r)

    if STAGE >= 3:
        texts = tbuf[...].astype(F32).reshape(X * nk * rows, width).astype(BF)
        images = ibuf[...].astype(F32).reshape(nq * no * rows, width).astype(BF)
        similarity = lax.dot_general(
            images, texts, (((1,), (1,)), ((), ())), preferred_element_type=F32
        )
        logits = scale * similarity + bias_ref[0]

        lane = lax.broadcasted_iota(jnp.int32, (rows, 128), 1)
        row = lax.broadcasted_iota(jnp.int32, (rows, 128), 0)
        pieces = []
        for q in range(nq):
            from_y = lax.rem(y - q // 2 + Y, Y)
            from_c = lax.rem(core + q % 2, 2)
            for step in IMAGE_STEPS:
                from_z = lax.rem(z - step + Z, Z)
                first = ((x * Y + from_y) * Z + from_z) * (2 * rows) + from_c * rows
                line = labels_ref[pl.ds(first // 128, 1), :]
                pick = lane == row + lax.rem(first, 128)
                pieces.append(jnp.where(pick, jnp.broadcast_to(line, (rows, 128)), 0))
        label = jnp.sum(jnp.concatenate(pieces, axis=0).astype(F32), axis=1, keepdims=True)

        spot = lax.broadcasted_iota(jnp.int32, (1, X * nk * rows), 1)
        at_row, at_k, at_j = spot % rows, (spot // rows) % nk, spot // (rows * nk)
        step_of = jnp.zeros_like(spot)
        for k, step in enumerate(TEXT_STEPS):
            step_of = jnp.where(at_k == k, step, step_of)
        from_x = lax.rem(x - at_j + X, X)
        from_z = lax.rem(z - side * step_of + Z, Z)
        column = (((from_x * Y + y) * Z + from_z) * 2 + core) * rows + at_row
        match = label == column.astype(F32)

        signed = jnp.where(match, -logits, logits)
        sigmoid = 1.0 / (1.0 + jnp.exp(-signed))
        weights = jnp.where(match, -sigmoid, sigmoid).astype(BF)

        grad = jnp.dot(weights, texts, preferred_element_type=F32)
        grad = grad.reshape(nq, no, rows, width)
        iown[...] = grad[0]
        isend[...] = grad[1:].astype(BF)
    low = lax.rem(z - IMAGE_STEPS[0] + Z, Z)
    first_image = (Z + 2 * STRIDE - 1 - low) // (2 * STRIDE)
    image_turns = [lax.rem(first_image + n, no) for n in range(no)]
    low = lax.rem(z - STRIDE + core + Z, Z)
    first_text = jnp.where(low > Z - nk, Z - low, 0)
    turn = [lax.rem(first_text + n, nk) for n in range(nk)]
    text_turns = [jnp.where(core == 0, n, nk - 1 - n) for n in turn]

    if STAGE >= 4:
        for o in image_turns:
            for q in range(1, nq):
                send(isend.at[q - 1, o], iback.at[o, q - 1], ri_s, ri_r.at[o],
                     device(dy=-(q // 2), dc=q % 2))
    if STAGE >= 3:
        grad = lax.dot_general(
            weights, images, (((0,), (0,)), ((), ())), preferred_element_type=F32
        )
        grad = grad.reshape(X, nk, rows, width)
        town[...] = grad[0]
        tsend[...] = grad[1:].astype(BF)
    if STAGE >= 4:
        for k in text_turns:
            for j in range(1, X):
                send(tsend.at[j - 1, k], tback.at[k, j - 1], rt_s, rt_r.at[k], device(dx=-j))

        def join_image(o):
            wait(iback.at[o], ri_r.at[o])
            total = iown[o] + jnp.sum(iback[o].astype(F32), axis=0)
            isum[o] = total.astype(BF)
            if STAGE >= 5:
                send(isum.at[o], ilast.at[o], li_s, li_r.at[o],
                     device(dz=2 * STRIDE * o - IMAGE_STEPS[0]))

        def join_text(k):
            wait(tback.at[k], rt_r.at[k])
            total = town[k] + jnp.sum(tback[k].astype(F32), axis=0)
            tsum[k] = total.astype(BF)

            @pl.when(k == home)
            def _():
                town[home] = total

            @pl.when(k != home)
            def _():
                if STAGE >= 5:
                    send(tsum.at[k], tlast.at[k], lt_s, lt_r.at[k], device(dz=side * (k - STRIDE)))

        join_image(image_turns[0])
        for n in range(nk):
            join_text(text_turns[n])
            if n == nk // 2:
                join_image(image_turns[1])
        for o in image_turns[2:]:
            join_image(o)

    def unit_back(unit, length, unit_grad):
        return (unit_grad - unit * jnp.sum(unit * unit_grad, axis=1, keepdims=True)) / length

    if STAGE >= 5:
        for o in range(no):
            wait(ilast.at[o], li_r.at[o])
        image_unit_grad = scale * jnp.sum(ilast[...].astype(F32), axis=0)
        image_out[...] = unit_back(image_unit, image_len, image_unit_grad)
        others = [k for k in range(nk) if k != home]
        for k in others:
            wait(tlast.at[k], lt_r.at[k])
        text_unit_grad = scale * sum((tlast[k].astype(F32) for k in others), town[home])
        text_out[...] = unit_back(text_unit, text_len, text_unit_grad)
    else:
        image_out[...] = image_unit
        text_out[...] = text_unit

    if STAGE >= 1:
        wait(ibuf.at[0], zi_s)
        wait(relay, zi_s)
        wait(tbuf.at[0, 1:], zt_s)
    if STAGE >= 2:
        wait(tbuf.at[1:], pt_s)
        wait(ibuf.at[1:], pi_s)
    if STAGE >= 4:
        wait(isend, ri_s)
        wait(tsend, rt_s)
    if STAGE >= 5:
        wait(isum, li_s)
        wait(tsum.at[1:], lt_s)


def per_device(image_emb, text_emb, labels, scale_logarithm, bias):
    rows, width = image_emb.shape
    nk, no, nq = len(TEXT_STEPS), len(IMAGE_STEPS), 2 * Y
    block = (rows, width)
    vmem = pl.BlockSpec(memory_space=pltpu.VMEM)
    hbm = pl.BlockSpec(memory_space=pltpu.HBM)
    one = pltpu.SemaphoreType.DMA
    some = lambda n: pltpu.SemaphoreType.DMA((n,))
    return pl.pallas_call(
        kernel,
        out_shape=[jax.ShapeDtypeStruct(block, F32)] * 2,
        in_specs=[hbm] * 5,
        out_specs=[vmem, vmem],
        scratch_shapes=[
            pltpu.VMEM(block, BF),
            pltpu.VMEM((X, nk) + block, BF),
            pltpu.VMEM((nq, no) + block, BF),
            pltpu.VMEM((X - 1, nk) + block, BF),
            pltpu.VMEM((nq - 1, no) + block, BF),
            pltpu.VMEM((nk,) + block, F32),
            pltpu.VMEM((no,) + block, F32),
            pltpu.VMEM((nk, X - 1) + block, BF),
            pltpu.VMEM((no, nq - 1) + block, BF),
            pltpu.VMEM((nk,) + block, BF),
            pltpu.VMEM((no,) + block, BF),
            pltpu.VMEM((nk,) + block, BF),
            pltpu.VMEM((no,) + block, BF),
            one, some(nk), one, some(no),
            one, one, one, one,
            one, some(nk), one, some(no),
            one, some(nk), one, some(no),
            pltpu.VMEM(block, F32),
            pltpu.VMEM(block, F32),
            pltpu.VMEM((labels.shape[0] // 128, 128), jnp.int32),
            pltpu.SMEM((1,), F32),
            pltpu.SMEM((1,), F32),
            some(5),
            pltpu.VMEM((2,) + block, BF),
            some(2),
        ],
        compiler_params=pltpu.CompilerParams(
            collective_id=0, has_side_effects=True, vmem_limit_bytes=60 * 2**20
        ),
    )(labels.reshape(-1, 128), scale_logarithm, bias, image_emb, text_emb)


def solution(mesh):
    rows = P(("outer", "inner"), None)
    return jax.shard_map(
        per_device,
        mesh=mesh,
        in_specs=(rows, rows, P(), P(), P()),
        out_specs=(rows, rows),
        check_vma=False,
    )
```

```python
import functools

import jax
import jax.numpy as jnp
from jax import lax
from jax.experimental import pallas as pl
from jax.experimental.pallas import tpu as pltpu
from jax.sharding import PartitionSpec as P

EPSILON = 1e-06
X, Y, Z = 4, 4, 32
STRIDE = 4
TEXT_STEPS = (4, 3, 2, 1, 0, -1, -2, -3)
IMAGE_STEPS = (12, 4, -4, -12)
BF = jnp.bfloat16
F32 = jnp.float32


def kernel(
    labels_hbm, scale_hbm, bias_hbm, image_hbm, text_hbm,
    image_out, text_out,
    own_image, tbuf, ibuf, tsend, isend, town, iown, tback, iback,
    tsum, isum, tlast, ilast,
    zt_s, zt_r, zi_s, zi_r, pt_s, pt_r, pi_s, pi_r,
    rt_s, rt_r, ri_s, ri_r, lt_s, lt_r, li_s, li_r,
    image_ref, text_ref, labels_ref, scale_ref, bias_ref, load, tnear, ready,
):
    nk, no = len(TEXT_STEPS), len(IMAGE_STEPS)
    nq = 2 * Y
    home = TEXT_STEPS.index(0)
    rows, width = image_ref.shape
    loads = [
        pltpu.make_async_copy(src, dst, load.at[n])
        for n, (src, dst) in enumerate(
            ((image_hbm, image_ref), (text_hbm, text_ref), (labels_hbm, labels_ref),
             (scale_hbm, scale_ref), (bias_hbm, bias_ref))
        )
    ]
    for copy in loads:
        copy.start()
    x = lax.axis_index("outer")
    inner = lax.axis_index("inner")
    core = lax.rem(inner, 2)
    z = lax.rem(inner // 2, Z)
    y = inner // (2 * Z)
    side = 1 - 2 * core

    def device(dx=0, dy=0, dz=0, dc=0):
        place_y = lax.rem(y + dy + Y, Y)
        place_z = lax.rem(z + dz + Z, Z)
        place_c = lax.rem(core + dc, 2)
        return (lax.rem(x + dx + X, X), (place_y * Z + place_z) * 2 + place_c)

    def send(src, dst, send_sem, recv_sem, place):
        pltpu.make_async_remote_copy(
            src_ref=src, dst_ref=dst, send_sem=send_sem, recv_sem=recv_sem,
            device_id=place, device_id_type=pl.DeviceIdType.MESH,
        ).start()

    def wait(ref, sem):
        pltpu.make_async_copy(ref, ref, sem).wait()

    barrier = pltpu.get_barrier_semaphore()
    near = {abs(s) for s in TEXT_STEPS if s}
    partners = [device(dz=d) for a in sorted(near, reverse=True) for d in {a % Z, -a % Z}]
    partners += [device(dx=j) for j in range(1, X)]
    partners += [device(dy=q // 2, dc=q % 2) for q in range(1, nq)]
    for place in partners:
        pl.semaphore_signal(barrier, inc=1, device_id=place, device_id_type=pl.DeviceIdType.MESH)

    def normalize(values):
        length = jnp.sqrt(jnp.sum(values * values, axis=1, keepdims=True) + EPSILON)
        return values / length, length

    for copy in loads:
        copy.wait()
    image_unit, image_len = normalize(image_ref[...])
    text_unit, text_len = normalize(text_ref[...])
    own_image[...] = image_unit.astype(BF)
    tbuf[0, home] = text_unit.astype(BF)
    scale = jnp.exp(jnp.full((1, 1), scale_ref[0], F32))

    pl.semaphore_wait(barrier, len(partners))

    def spread_text(k):
        for j in range(1, X):
            send(tbuf.at[0, k], tbuf.at[j, k], pt_s, pt_r, device(dx=j))

    def spread_image(o):
        for q in range(1, nq):
            send(ibuf.at[o, 0], ibuf.at[o, q], pi_s, pi_r.at[o], device(dy=q // 2, dc=q % 2))

    for o, step in ((1, STRIDE), (2, -STRIDE)):
        send(own_image, ibuf.at[o, 0], zi_s, zi_r.at[o], device(dz=step))
        pl.semaphore_signal(
            ready.at[2 - o], inc=1, device_id=device(dz=step),
            device_id_type=pl.DeviceIdType.MESH,
        )
    for k, step in sorted(enumerate(TEXT_STEPS), key=lambda w: abs(w[1])):
        if step:
            send(tbuf.at[0, home], tbuf.at[0, k], zt_s, zt_r.at[k], device(dz=side * step))
    spread_text(home)

    lane = lax.broadcasted_iota(jnp.int32, (rows, 128), 1)
    row = lax.broadcasted_iota(jnp.int32, (rows, 128), 0)

    def label_of(step):
        pieces = []
        for q in range(nq):
            from_y = lax.rem(y - q // 2 + Y, Y)
            from_c = lax.rem(core + q % 2, 2)
            from_z = lax.rem(z - step + Z, Z)
            first = ((x * Y + from_y) * Z + from_z) * (2 * rows) + from_c * rows
            line = labels_ref[pl.ds(first // 128, 1), :]
            pick = lane == row + lax.rem(first, 128)
            pieces.append(jnp.where(pick, jnp.broadcast_to(line, (rows, 128)), 0))
        pieces = jnp.concatenate(pieces, axis=0).astype(F32)
        return jnp.sum(pieces, axis=1, keepdims=True)

    swap = lax.rem(z + IMAGE_STEPS[0], Z) < lax.rem(z - IMAGE_STEPS[0] + Z, Z)
    far_turns = [jnp.where(swap, 3, 0), jnp.where(swap, 0, 3)]
    near_label = jnp.concatenate([label_of(STRIDE), label_of(-STRIDE)], axis=0)
    far_labels = [label_of(IMAGE_STEPS[0] - 2 * STRIDE * o) for o in far_turns]

    spot = lax.broadcasted_iota(jnp.int32, (1, X * nk * rows), 1)
    at_row, at_k, at_j = spot % rows, (spot // rows) % nk, spot // (rows * nk)
    from_x = lax.rem(x - at_j + X, X)
    from_z = lax.rem(z - side * (STRIDE - at_k) + Z, Z)
    column = (((from_x * Y + y) * Z + from_z) * 2 + core) * rows + at_row
    column = column.astype(F32)

    def as_rows(block):
        return block.astype(F32).reshape(-1, width).astype(BF)

    def weigh(images, texts, label):
        similarity = lax.dot_general(
            images, texts, (((1,), (1,)), ((), ())), preferred_element_type=F32
        )
        logits = scale * similarity + bias_ref[0]
        match = label == column
        signed = jnp.where(match, -logits, logits)
        sigmoid = 1.0 / (1.0 + jnp.exp(-signed))
        return jnp.where(match, -sigmoid, sigmoid).astype(BF)

    def keep_images(grad, slots):
        grad = grad.reshape(len(slots), nq, rows, width)
        for n, o in enumerate(slots):
            iown[o] = grad[n, 0]
            isend[o] = grad[n, 1:].astype(BF)

    def return_image(o):
        for q in range(1, nq):
            send(isend.at[o, q - 1], iback.at[o, q - 1], ri_s, ri_r.at[o],
                 device(dy=-(q // 2), dc=q % 2))

    def join_image(o):
        wait(iback.at[o], ri_r.at[o])
        total = iown[o] + jnp.sum(iback[o].astype(F32), axis=0)
        isum[o] = total.astype(BF)
        send(isum.at[o], ilast.at[o], li_s, li_r.at[o],
             device(dz=2 * STRIDE * o - IMAGE_STEPS[0]))

    def pull_text(k):
        wait(tbuf.at[0, k], zt_r.at[k])
        spread_text(k)

    for k, step in enumerate(TEXT_STEPS):
        if 0 < abs(step) <= STRIDE // 2:
            pull_text(k)
    for o, step in ((1, STRIDE), (2, -STRIDE)):
        wait(ibuf.at[o, 0], zi_r.at[o])
        pl.semaphore_wait(ready.at[o - 1], 1)
        far = 0 if o == 1 else 3
        send(ibuf.at[o, 0], ibuf.at[far, 0], zi_s, zi_r.at[far], device(dz=2 * step))
    for o in (1, 2):
        spread_image(o)
    for k, step in enumerate(TEXT_STEPS):
        if STRIDE // 2 < abs(step):
            pull_text(k)

    def pull_far():
        for o in far_turns:
            wait(ibuf.at[o, 0], zi_r.at[o])
            spread_image(o)

    pull_far()

    wait(tbuf.at[1:], pt_r)
    for o in (1, 2):
        wait(ibuf.at[o, 1:], pi_r.at[o])
    texts = as_rows(tbuf[...])
    images = as_rows(ibuf[1:3])
    weights = weigh(images, texts, near_label)
    keep_images(jnp.dot(weights, texts, preferred_element_type=F32), (1, 2))
    return_image(1)
    return_image(2)
    tnear[...] = lax.dot_general(
        weights, images, (((0,), (0,)), ((), ())), preferred_element_type=F32
    )
    urgent_low = jnp.logical_and(z >= STRIDE, z < 3 * STRIDE)
    urgent_high = jnp.logical_or(z < STRIDE, z >= Z - STRIDE)
    urgent_far = jnp.logical_and(z >= 3 * STRIDE, z < Z - STRIDE)

    for n, o in enumerate(far_turns):
        wait(ibuf.at[o, 1:], pi_r.at[o])
        images = as_rows(ibuf[o])
        weights = weigh(images, texts, far_labels[n])
        keep_images(jnp.dot(weights, texts, preferred_element_type=F32), (o,))
        return_image(o)
        tnear[...] += lax.dot_general(
            weights, images, (((0,), (0,)), ((), ())), preferred_element_type=F32
        )

    low = lax.rem(z - STRIDE + core + Z, Z)
    first_text = jnp.where(low > Z - nk, Z - low, 0)
    turn = [lax.rem(first_text + n, nk) for n in range(nk)]
    text_turns = [jnp.where(core == 0, n, nk - 1 - n) for n in turn]

    grad = tnear[...].reshape(X, nk, rows, width)
    town[...] = grad[0]
    tsend[...] = grad[1:].astype(BF)
    for k in text_turns:
        for j in range(1, X):
            send(tsend.at[j - 1, k], tback.at[k, j - 1], rt_s, rt_r.at[k], device(dx=-j))

    def join_text(k):
        wait(tback.at[k], rt_r.at[k])
        total = town[k] + jnp.sum(tback[k].astype(F32), axis=0)
        tsum[k] = total.astype(BF)

        @pl.when(k == home)
        def _():
            town[home] = total

        @pl.when(k != home)
        def _():
            send(tsum.at[k], tlast.at[k], lt_s, lt_r.at[k], device(dz=side * (k - STRIDE)))

    @pl.when(urgent_far)
    def _():
        join_image(far_turns[0])

    @pl.when(urgent_low)
    def _():
        join_image(1)

    @pl.when(urgent_high)
    def _():
        join_image(2)

    for n in range(nk):
        join_text(text_turns[n])

    @pl.when(jnp.logical_not(urgent_far))
    def _():
        join_image(far_turns[0])

    join_image(far_turns[1])

    @pl.when(jnp.logical_not(urgent_low))
    def _():
        join_image(1)

    @pl.when(jnp.logical_not(urgent_high))
    def _():
        join_image(2)

    def unit_back(unit, length, unit_grad):
        return (unit_grad - unit * jnp.sum(unit * unit_grad, axis=1, keepdims=True)) / length

    for o in range(no):
        wait(ilast.at[o], li_r.at[o])
    image_unit_grad = scale * jnp.sum(ilast[...].astype(F32), axis=0)
    image_out[...] = unit_back(image_unit, image_len, image_unit_grad)
    others = [k for k in range(nk) if k != home]
    for k in others:
        wait(tlast.at[k], lt_r.at[k])
    text_unit_grad = scale * sum((tlast[k].astype(F32) for k in others), town[home])
    text_out[...] = unit_back(text_unit, text_len, text_unit_grad)
    wait(isum, zi_s)
    wait(tbuf.at[0, 1:], zt_s)
    wait(tbuf.at[1:], pt_s)
    wait(iback, pi_s)
    wait(isend, ri_s)
    wait(tsend, rt_s)
    wait(isum, li_s)
    wait(tsum.at[1:], lt_s)


def per_device(image_emb, text_emb, labels, scale_logarithm, bias):
    rows, width = image_emb.shape
    nk, no, nq = len(TEXT_STEPS), len(IMAGE_STEPS), 2 * Y
    block = (rows, width)
    vmem = pl.BlockSpec(memory_space=pltpu.VMEM)
    hbm = pl.BlockSpec(memory_space=pltpu.HBM)
    one = pltpu.SemaphoreType.DMA
    some = lambda n: pltpu.SemaphoreType.DMA((n,))
    return pl.pallas_call(
        kernel,
        out_shape=[jax.ShapeDtypeStruct(block, F32)] * 2,
        in_specs=[hbm] * 5,
        out_specs=[vmem, vmem],
        scratch_shapes=[
            pltpu.VMEM(block, BF),
            pltpu.VMEM((X, nk) + block, BF),
            pltpu.VMEM((no, nq) + block, BF),
            pltpu.VMEM((X - 1, nk) + block, BF),
            pltpu.VMEM((no, nq - 1) + block, BF),
            pltpu.VMEM((nk,) + block, F32),
            pltpu.VMEM((no,) + block, F32),
            pltpu.VMEM((nk, X - 1) + block, BF),
            pltpu.VMEM((no, nq - 1) + block, BF),
            pltpu.VMEM((nk,) + block, BF),
            pltpu.VMEM((no,) + block, BF),
            pltpu.VMEM((nk,) + block, BF),
            pltpu.VMEM((no,) + block, BF),
            one, some(nk), one, some(no),
            one, one, one, some(no),
            one, some(nk), one, some(no),
            one, some(nk), one, some(no),
            pltpu.VMEM(block, F32),
            pltpu.VMEM(block, F32),
            pltpu.VMEM((labels.shape[0] // 128, 128), jnp.int32),
            pltpu.SMEM((1,), F32),
            pltpu.SMEM((1,), F32),
            some(5),
            pltpu.VMEM((X * nk * rows, width), F32),
            pltpu.SemaphoreType.REGULAR((2,)),
        ],
        compiler_params=pltpu.CompilerParams(
            collective_id=0, has_side_effects=True, vmem_limit_bytes=60 * 2**20
        ),
    )(labels.reshape(-1, 128), scale_logarithm, bias, image_emb, text_emb)


def solution(mesh):
    rows = P(("outer", "inner"), None)
    return jax.shard_map(
        per_device,
        mesh=mesh,
        in_specs=(rows, rows, P(), P(), P()),
        out_specs=(rows, rows),
        check_vma=False,
    )
```

```python
import functools

import jax
import jax.numpy as jnp
from jax import lax
from jax.experimental import pallas as pl
from jax.experimental.pallas import tpu as pltpu
from jax.sharding import PartitionSpec as P

EPSILON = 1e-06
X, Y, Z = 4, 4, 32
STRIDE = 4
TEXT_STEPS = (4, 3, 2, 1, 0, -1, -2, -3)
IMAGE_STEPS = (12, 4, -4, -12)
BF = jnp.bfloat16
F32 = jnp.float32


def kernel(
    labels_hbm, scale_hbm, bias_hbm, image_hbm, text_hbm,
    image_out, text_out,
    own_image, tbuf, ibuf, tsend, isend, town, iown, tback, iback,
    tsum, isum, tlast, ilast,
    zt_s, zt_r, zi_s, zi_r, pt_s, pt_r, pi_s, pi_r,
    rt_s, rt_r, ri_s, ri_r, lt_s, lt_r, li_s, li_r,
    image_ref, text_ref, labels_ref, scale_ref, bias_ref, load, tnear, ready,
):
    nk, no = len(TEXT_STEPS), len(IMAGE_STEPS)
    nq = 2 * Y
    home = TEXT_STEPS.index(0)
    rows, width = image_ref.shape
    loads = [
        pltpu.make_async_copy(src, dst, load.at[n])
        for n, (src, dst) in enumerate(
            ((image_hbm, image_ref), (text_hbm, text_ref), (labels_hbm, labels_ref),
             (scale_hbm, scale_ref), (bias_hbm, bias_ref))
        )
    ]
    for copy in loads:
        copy.start()
    x = lax.axis_index("outer")
    inner = lax.axis_index("inner")
    core = lax.rem(inner, 2)
    z = lax.rem(inner // 2, Z)
    y = inner // (2 * Z)
    side = 1 - 2 * core

    def device(dx=0, dy=0, dz=0, dc=0):
        place_y = lax.rem(y + dy + Y, Y)
        place_z = lax.rem(z + dz + Z, Z)
        place_c = lax.rem(core + dc, 2)
        return (lax.rem(x + dx + X, X), (place_y * Z + place_z) * 2 + place_c)

    def send(src, dst, send_sem, recv_sem, place):
        pltpu.make_async_remote_copy(
            src_ref=src, dst_ref=dst, send_sem=send_sem, recv_sem=recv_sem,
            device_id=place, device_id_type=pl.DeviceIdType.MESH,
        ).start()

    def wait(ref, sem):
        pltpu.make_async_copy(ref, ref, sem).wait()

    barrier = pltpu.get_barrier_semaphore()
    near = {abs(s) for s in TEXT_STEPS if s}
    partners = [device(dz=d) for a in sorted(near, reverse=True) for d in {a % Z, -a % Z}]
    partners += [device(dx=j) for j in range(1, X)]
    partners += [device(dy=q // 2, dc=q % 2) for q in range(1, nq)]
    for place in partners:
        pl.semaphore_signal(barrier, inc=1, device_id=place, device_id_type=pl.DeviceIdType.MESH)

    def normalize(values):
        length = jnp.sqrt(jnp.sum(values * values, axis=1, keepdims=True) + EPSILON)
        return values / length, length

    for copy in loads:
        copy.wait()
    image_unit, image_len = normalize(image_ref[...])
    text_unit, text_len = normalize(text_ref[...])
    own_image[...] = image_unit.astype(BF)
    tbuf[0, home] = text_unit.astype(BF)
    scale = jnp.exp(jnp.full((1, 1), scale_ref[0], F32))

    pl.semaphore_wait(barrier, len(partners))

    def spread_text(k):
        for j in range(1, X):
            send(tbuf.at[0, k], tbuf.at[j, k], pt_s, pt_r, device(dx=j))

    def spread_image(o):
        for q in range(1, nq):
            send(ibuf.at[o, 0], ibuf.at[o, q], pi_s, pi_r.at[o], device(dy=q // 2, dc=q % 2))

    for o, step in ((1, STRIDE), (2, -STRIDE)):
        send(own_image, ibuf.at[o, 0], zi_s, zi_r.at[o], device(dz=step))
        pl.semaphore_signal(
            ready.at[2 - o], inc=1, device_id=device(dz=step),
            device_id_type=pl.DeviceIdType.MESH,
        )
    for k, step in sorted(enumerate(TEXT_STEPS), key=lambda w: abs(w[1])):
        if step:
            send(tbuf.at[0, home], tbuf.at[0, k], zt_s, zt_r.at[k], device(dz=side * step))
        else:
            spread_text(home)

    urgent_low = jnp.logical_and(z >= STRIDE, z < 3 * STRIDE)
    urgent_high = jnp.logical_or(z < STRIDE, z >= Z - STRIDE)
    urgent_far = jnp.logical_and(z >= 3 * STRIDE, z < Z - STRIDE)

    lane = lax.broadcasted_iota(jnp.int32, (rows, 128), 1)
    row = lax.broadcasted_iota(jnp.int32, (rows, 128), 0)

    def label_of(step):
        pieces = []
        for q in range(nq):
            from_y = lax.rem(y - q // 2 + Y, Y)
            from_c = lax.rem(core + q % 2, 2)
            from_z = lax.rem(z - step + Z, Z)
            first = ((x * Y + from_y) * Z + from_z) * (2 * rows) + from_c * rows
            line = labels_ref[pl.ds(first // 128, 1), :]
            pick = lane == row + lax.rem(first, 128)
            pieces.append(jnp.where(pick, jnp.broadcast_to(line, (rows, 128)), 0))
        pieces = jnp.concatenate(pieces, axis=0).astype(F32)
        return jnp.sum(pieces, axis=1, keepdims=True)

    swap = lax.rem(z + IMAGE_STEPS[0], Z) < lax.rem(z - IMAGE_STEPS[0] + Z, Z)
    far_turns = [jnp.where(swap, 3, 0), jnp.where(swap, 0, 3)]
    near_label = jnp.concatenate([label_of(STRIDE), label_of(-STRIDE)], axis=0)
    far_labels = [label_of(IMAGE_STEPS[0] - 2 * STRIDE * o) for o in far_turns]

    spot = lax.broadcasted_iota(jnp.int32, (1, X * nk * rows), 1)
    at_row, at_k, at_j = spot % rows, (spot // rows) % nk, spot // (rows * nk)
    from_x = lax.rem(x - at_j + X, X)
    from_z = lax.rem(z - side * (STRIDE - at_k) + Z, Z)
    column = (((from_x * Y + y) * Z + from_z) * 2 + core) * rows + at_row
    column = column.astype(F32)

    def as_rows(block):
        return block.astype(F32).reshape(-1, width).astype(BF)

    def weigh(images, texts, label):
        similarity = lax.dot_general(
            images, texts, (((1,), (1,)), ((), ())), preferred_element_type=F32
        )
        logits = scale * similarity + bias_ref[0]
        match = label == column
        signed = jnp.where(match, -logits, logits)
        sigmoid = 1.0 / (1.0 + jnp.exp(-signed))
        return jnp.where(match, -sigmoid, sigmoid).astype(BF)

    def keep_images(grad, slots):
        grad = grad.reshape(len(slots), nq, rows, width)
        for n, o in enumerate(slots):
            iown[o] = grad[n, 0]
            isend[o] = grad[n, 1:].astype(BF)

    def return_image(o):
        for q in range(1, nq):
            send(isend.at[o, q - 1], iback.at[o, q - 1], ri_s, ri_r.at[o],
                 device(dy=-(q // 2), dc=q % 2))

    def join_image(o):
        wait(iback.at[o], ri_r.at[o])
        total = iown[o] + jnp.sum(iback[o].astype(F32), axis=0)
        isum[o] = total.astype(BF)
        send(isum.at[o], ilast.at[o], li_s, li_r.at[o],
             device(dz=2 * STRIDE * o - IMAGE_STEPS[0]))

    def pull_text(k):
        wait(tbuf.at[0, k], zt_r.at[k])
        spread_text(k)

    for k, step in sorted(enumerate(TEXT_STEPS), key=lambda w: abs(w[1])):
        if 0 < abs(step) <= STRIDE // 2:
            pull_text(k)
    start = jnp.where(urgent_high, 2, 1)
    for o in (start, 3 - start):
        step = STRIDE * (3 - 2 * o)
        wait(ibuf.at[o, 0], zi_r.at[o])
        pl.semaphore_wait(ready.at[o - 1], 1)
        far = 3 * (o - 1)
        send(ibuf.at[o, 0], ibuf.at[far, 0], zi_s, zi_r.at[far], device(dz=2 * step))
    for k, step in sorted(enumerate(TEXT_STEPS), key=lambda w: abs(w[1])):
        if abs(step) > STRIDE // 2:
            pull_text(k)
    for o in (1, 2):
        spread_image(o)

    def pull_far():
        for o in far_turns:
            wait(ibuf.at[o, 0], zi_r.at[o])
            spread_image(o)

    pull_far()

    wait(tbuf.at[1:], pt_r)
    for o in (1, 2):
        wait(ibuf.at[o, 1:], pi_r.at[o])
    texts = as_rows(tbuf[...])
    images = as_rows(ibuf[1:3])
    weights = weigh(images, texts, near_label)
    keep_images(jnp.dot(weights, texts, preferred_element_type=F32), (1, 2))
    return_image(1)
    return_image(2)
    tnear[...] = lax.dot_general(
        weights, images, (((0,), (0,)), ((), ())), preferred_element_type=F32
    )
    for n, o in enumerate(far_turns):
        wait(ibuf.at[o, 1:], pi_r.at[o])
        images = as_rows(ibuf[o])
        weights = weigh(images, texts, far_labels[n])
        keep_images(jnp.dot(weights, texts, preferred_element_type=F32), (o,))
        return_image(o)
        tnear[...] += lax.dot_general(
            weights, images, (((0,), (0,)), ((), ())), preferred_element_type=F32
        )

    low = lax.rem(z - STRIDE + core + Z, Z)
    first_text = jnp.where(low > Z - nk, Z - low, 0)
    turn = [lax.rem(first_text + n, nk) for n in range(nk)]
    text_turns = [jnp.where(core == 0, n, nk - 1 - n) for n in turn]

    grad = tnear[...].reshape(X, nk, rows, width)
    town[...] = grad[0]
    tsend[...] = grad[1:].astype(BF)
    for k in text_turns:
        for j in range(1, X):
            send(tsend.at[j - 1, k], tback.at[k, j - 1], rt_s, rt_r.at[k], device(dx=-j))

    def join_text(k):
        wait(tback.at[k], rt_r.at[k])
        total = town[k] + jnp.sum(tback[k].astype(F32), axis=0)
        tsum[k] = total.astype(BF)

        @pl.when(k == home)
        def _():
            town[home] = total

        @pl.when(k != home)
        def _():
            send(tsum.at[k], tlast.at[k], lt_s, lt_r.at[k], device(dz=side * (k - STRIDE)))

    @pl.when(urgent_far)
    def _():
        join_image(far_turns[0])

    @pl.when(urgent_low)
    def _():
        join_image(1)

    @pl.when(urgent_high)
    def _():
        join_image(2)

    for n in range(nk):
        join_text(text_turns[n])

    @pl.when(jnp.logical_not(urgent_far))
    def _():
        join_image(far_turns[0])

    join_image(far_turns[1])

    @pl.when(jnp.logical_not(urgent_low))
    def _():
        join_image(1)

    @pl.when(jnp.logical_not(urgent_high))
    def _():
        join_image(2)

    def unit_back(unit, length, unit_grad):
        return (unit_grad - unit * jnp.sum(unit * unit_grad, axis=1, keepdims=True)) / length

    for o in range(no):
        wait(ilast.at[o], li_r.at[o])
    image_unit_grad = scale * jnp.sum(ilast[...].astype(F32), axis=0)
    image_out[...] = unit_back(image_unit, image_len, image_unit_grad)
    others = [k for k in range(nk) if k != home]
    for k in others:
        wait(tlast.at[k], lt_r.at[k])
    text_unit_grad = scale * sum((tlast[k].astype(F32) for k in others), town[home])
    text_out[...] = unit_back(text_unit, text_len, text_unit_grad)
    wait(isum, zi_s)
    wait(tbuf.at[0, 1:], zt_s)
    wait(tbuf.at[1:], pt_s)
    wait(iback, pi_s)
    wait(isend, ri_s)
    wait(tsend, rt_s)
    wait(isum, li_s)
    wait(tsum.at[1:], lt_s)


def per_device(image_emb, text_emb, labels, scale_logarithm, bias):
    rows, width = image_emb.shape
    nk, no, nq = len(TEXT_STEPS), len(IMAGE_STEPS), 2 * Y
    block = (rows, width)
    vmem = pl.BlockSpec(memory_space=pltpu.VMEM)
    hbm = pl.BlockSpec(memory_space=pltpu.HBM)
    one = pltpu.SemaphoreType.DMA
    some = lambda n: pltpu.SemaphoreType.DMA((n,))
    return pl.pallas_call(
        kernel,
        out_shape=[jax.ShapeDtypeStruct(block, F32)] * 2,
        in_specs=[hbm] * 5,
        out_specs=[vmem, vmem],
        scratch_shapes=[
            pltpu.VMEM(block, BF),
            pltpu.VMEM((X, nk) + block, BF),
            pltpu.VMEM((no, nq) + block, BF),
            pltpu.VMEM((X - 1, nk) + block, BF),
            pltpu.VMEM((no, nq - 1) + block, BF),
            pltpu.VMEM((nk,) + block, F32),
            pltpu.VMEM((no,) + block, F32),
            pltpu.VMEM((nk, X - 1) + block, BF),
            pltpu.VMEM((no, nq - 1) + block, BF),
            pltpu.VMEM((nk,) + block, BF),
            pltpu.VMEM((no,) + block, BF),
            pltpu.VMEM((nk,) + block, BF),
            pltpu.VMEM((no,) + block, BF),
            one, some(nk), one, some(no),
            one, one, one, some(no),
            one, some(nk), one, some(no),
            one, some(nk), one, some(no),
            pltpu.VMEM(block, F32),
            pltpu.VMEM(block, F32),
            pltpu.VMEM((labels.shape[0] // 128, 128), jnp.int32),
            pltpu.SMEM((1,), F32),
            pltpu.SMEM((1,), F32),
            some(5),
            pltpu.VMEM((X * nk * rows, width), F32),
            pltpu.SemaphoreType.REGULAR((2,)),
        ],
        compiler_params=pltpu.CompilerParams(
            collective_id=0, has_side_effects=True, vmem_limit_bytes=55112 * 1024
        ),
    )(labels.reshape(-1, 128), scale_logarithm, bias, image_emb, text_emb)


def solution(mesh):
    rows = P(("outer", "inner"), None)
    return jax.shard_map(
        per_device,
        mesh=mesh,
        in_specs=(rows, rows, P(), P(), P()),
        out_specs=(rows, rows),
        check_vma=False,
    )
```

```python
import functools

import jax
import jax.numpy as jnp
from jax import lax
from jax.experimental import pallas as pl
from jax.experimental.pallas import tpu as pltpu
from jax.sharding import PartitionSpec as P

EPSILON = 1e-06
X, Y, Z = 4, 4, 32
STRIDE = 4
TEXT_STEPS = (4, 3, 2, 1, 0, -1, -2, -3)
IMAGE_STEPS = (12, 4, -4, -12)
BF = jnp.bfloat16
F32 = jnp.float32


def kernel(
    labels_hbm, scale_hbm, bias_hbm, image_hbm, text_hbm,
    image_out, text_out,
    own_image, tbuf, ibuf, tsend, isend, town, iown, tback, iback,
    tsum, isum, tlast, ilast,
    zt_s, zt_r, zi_s, zi_r, pt_s, pt_r, pi_s, pi_r,
    rt_s, rt_r, ri_s, ri_r, lt_s, lt_r, li_s, li_r,
    image_ref, text_ref, labels_ref, scale_ref, bias_ref, load, tnear, ready,
):
    nk, no = len(TEXT_STEPS), len(IMAGE_STEPS)
    nq = 2 * Y
    home = TEXT_STEPS.index(0)
    rows, width = image_ref.shape
    loads = [
        pltpu.make_async_copy(src, dst, load.at[n])
        for n, (src, dst) in enumerate(
            ((image_hbm, image_ref), (text_hbm, text_ref), (labels_hbm, labels_ref),
             (scale_hbm, scale_ref), (bias_hbm, bias_ref))
        )
    ]
    for copy in loads:
        copy.start()
    x = lax.axis_index("outer")
    inner = lax.axis_index("inner")
    core = lax.rem(inner, 2)
    z = lax.rem(inner // 2, Z)
    y = inner // (2 * Z)
    side = 1 - 2 * core

    def device(dx=0, dy=0, dz=0, dc=0):
        place_y = lax.rem(y + dy + Y, Y)
        place_z = lax.rem(z + dz + Z, Z)
        place_c = lax.rem(core + dc, 2)
        return (lax.rem(x + dx + X, X), (place_y * Z + place_z) * 2 + place_c)

    def send(src, dst, send_sem, recv_sem, place):
        pltpu.make_async_remote_copy(
            src_ref=src, dst_ref=dst, send_sem=send_sem, recv_sem=recv_sem,
            device_id=place, device_id_type=pl.DeviceIdType.MESH,
        ).start()

    def wait(ref, sem):
        pltpu.make_async_copy(ref, ref, sem).wait()

    barrier = pltpu.get_barrier_semaphore()
    near = {abs(s) for s in TEXT_STEPS if s}
    partners = [device(dz=d) for a in sorted(near, reverse=True) for d in {a % Z, -a % Z}]
    partners += [device(dx=j) for j in range(1, X)]
    partners += [device(dy=q // 2, dc=q % 2) for q in range(1, nq)]
    for place in partners:
        pl.semaphore_signal(barrier, inc=1, device_id=place, device_id_type=pl.DeviceIdType.MESH)

    def normalize(values):
        length = jnp.sqrt(jnp.sum(values * values, axis=1, keepdims=True) + EPSILON)
        return values / length, length

    for copy in loads:
        copy.wait()
    image_unit, image_len = normalize(image_ref[...])
    text_unit, text_len = normalize(text_ref[...])
    own_image[...] = image_unit.astype(BF)
    tbuf[0, home] = text_unit.astype(BF)
    scale = jnp.exp(jnp.full((1, 1), scale_ref[0], F32))

    pl.semaphore_wait(barrier, len(partners))

    def spread_text(k):
        for j in range(1, X):
            send(tbuf.at[0, k], tbuf.at[j, k], pt_s, pt_r, device(dx=j))

    def spread_image(o):
        for q in range(1, nq):
            send(ibuf.at[o, 0], ibuf.at[o, q], pi_s, pi_r.at[o], device(dy=q // 2, dc=q % 2))

    for o, step in ((1, STRIDE), (2, -STRIDE)):
        send(own_image, ibuf.at[o, 0], zi_s, zi_r.at[o], device(dz=step))
        pl.semaphore_signal(
            ready.at[2 - o], inc=1, device_id=device(dz=step),
            device_id_type=pl.DeviceIdType.MESH,
        )
    for k, step in sorted(enumerate(TEXT_STEPS), key=lambda w: abs(w[1])):
        if step:
            send(tbuf.at[0, home], tbuf.at[0, k], zt_s, zt_r.at[k], device(dz=side * step))
        else:
            spread_text(home)

    urgent_low = jnp.logical_and(z >= STRIDE, z < 3 * STRIDE)
    urgent_high = jnp.logical_or(z < STRIDE, z >= Z - STRIDE)
    urgent_far = jnp.logical_and(z >= 3 * STRIDE, z < Z - STRIDE)

    lane = lax.broadcasted_iota(jnp.int32, (rows, 128), 1)
    row = lax.broadcasted_iota(jnp.int32, (rows, 128), 0)

    def label_of(step):
        pieces = []
        for q in range(nq):
            from_y = lax.rem(y - q // 2 + Y, Y)
            from_c = lax.rem(core + q % 2, 2)
            from_z = lax.rem(z - step + Z, Z)
            first = ((x * Y + from_y) * Z + from_z) * (2 * rows) + from_c * rows
            line = labels_ref[pl.ds(first // 128, 1), :]
            pick = lane == row + lax.rem(first, 128)
            pieces.append(jnp.where(pick, jnp.broadcast_to(line, (rows, 128)), 0))
        pieces = jnp.concatenate(pieces, axis=0).astype(F32)
        return jnp.sum(pieces, axis=1, keepdims=True)

    swap = lax.rem(z + IMAGE_STEPS[0], Z) < lax.rem(z - IMAGE_STEPS[0] + Z, Z)
    far_turns = [jnp.where(swap, 3, 0), jnp.where(swap, 0, 3)]
    near_label = jnp.concatenate([label_of(STRIDE), label_of(-STRIDE)], axis=0)
    far_labels = [label_of(IMAGE_STEPS[0] - 2 * STRIDE * o) for o in far_turns]

    spot = lax.broadcasted_iota(jnp.int32, (1, X * nk * rows), 1)
    at_row, at_k, at_j = spot % rows, (spot // rows) % nk, spot // (rows * nk)
    from_x = lax.rem(x - at_j + X, X)
    from_z = lax.rem(z - side * (STRIDE - at_k) + Z, Z)
    column = (((from_x * Y + y) * Z + from_z) * 2 + core) * rows + at_row
    column = column.astype(F32)

    def as_rows(block):
        return block.astype(F32).reshape(-1, width).astype(BF)

    def weigh(images, texts, label):
        similarity = lax.dot_general(
            images, texts, (((1,), (1,)), ((), ())), preferred_element_type=F32
        )
        logits = scale * similarity + bias_ref[0]
        match = label == column
        signed = jnp.where(match, -logits, logits)
        sigmoid = 1.0 / (1.0 + jnp.exp(-signed))
        return jnp.where(match, -sigmoid, sigmoid).astype(BF)

    def keep_images(grad, slots):
        grad = grad.reshape(len(slots), nq, rows, width)
        for n, o in enumerate(slots):
            iown[o] = grad[n, 0]
            isend[o] = grad[n, 1:].astype(BF)

    def return_image(o):
        for q in range(1, nq):
            send(isend.at[o, q - 1], iback.at[o, q - 1], ri_s, ri_r.at[o],
                 device(dy=-(q // 2), dc=q % 2))

    def join_image(o):
        wait(iback.at[o], ri_r.at[o])
        total = iown[o] + jnp.sum(iback[o].astype(F32), axis=0)
        isum[o] = total.astype(BF)
        send(isum.at[o], ilast.at[o], li_s, li_r.at[o],
             device(dz=2 * STRIDE * o - IMAGE_STEPS[0]))

    def pull_text(k):
        wait(tbuf.at[0, k], zt_r.at[k])
        spread_text(k)

    for k, step in sorted(enumerate(TEXT_STEPS), key=lambda w: abs(w[1])):
        if 0 < abs(step) <= STRIDE // 2:
            pull_text(k)
    start = jnp.where(urgent_high, 2, 1)
    for o in (start, 3 - start):
        step = STRIDE * (3 - 2 * o)
        wait(ibuf.at[o, 0], zi_r.at[o])
        pl.semaphore_wait(ready.at[o - 1], 1)
        far = 3 * (o - 1)
        send(ibuf.at[o, 0], ibuf.at[far, 0], zi_s, zi_r.at[far], device(dz=2 * step))
    for k, step in sorted(enumerate(TEXT_STEPS), key=lambda w: abs(w[1])):
        if abs(step) > STRIDE // 2:
            pull_text(k)
    for o in (1, 2):
        spread_image(o)

    def pull_far():
        for o in far_turns:
            wait(ibuf.at[o, 0], zi_r.at[o])
            spread_image(o)

    pull_far()

    wait(tbuf.at[1:], pt_r)
    for o in (1, 2):
        wait(ibuf.at[o, 1:], pi_r.at[o])
    texts = as_rows(tbuf[...])
    images = as_rows(ibuf[1:3])
    weights = weigh(images, texts, near_label)
    keep_images(jnp.dot(weights, texts, preferred_element_type=F32), (1, 2))
    tnear[...] = lax.dot_general(
        weights, images, (((0,), (0,)), ((), ())), preferred_element_type=F32
    )
    for n, o in enumerate(far_turns):
        wait(ibuf.at[o, 1:], pi_r.at[o])
        images = as_rows(ibuf[o])
        weights = weigh(images, texts, far_labels[n])
        keep_images(jnp.dot(weights, texts, preferred_element_type=F32), (o,))
        return_image(o)
        if n == 1:
            return_image(start)
            return_image(3 - start)
        tnear[...] += lax.dot_general(
            weights, images, (((0,), (0,)), ((), ())), preferred_element_type=F32
        )

    low = lax.rem(z - STRIDE + core + Z, Z)
    first_text = jnp.where(low > Z - nk, Z - low, 0)
    turn = [lax.rem(first_text + n, nk) for n in range(nk)]
    text_turns = [jnp.where(core == 0, n, nk - 1 - n) for n in turn]

    grad = tnear[...].reshape(X, nk, rows, width)
    town[...] = grad[0]
    tsend[...] = grad[1:].astype(BF)
    for k in text_turns:
        for j in range(1, X):
            send(tsend.at[j - 1, k], tback.at[k, j - 1], rt_s, rt_r.at[k], device(dx=-j))

    def join_text(k):
        wait(tback.at[k], rt_r.at[k])
        total = town[k] + jnp.sum(tback[k].astype(F32), axis=0)
        tsum[k] = total.astype(BF)

        @pl.when(k == home)
        def _():
            town[home] = total

        @pl.when(k != home)
        def _():
            send(tsum.at[k], tlast.at[k], lt_s, lt_r.at[k], device(dz=side * (k - STRIDE)))

    @pl.when(urgent_far)
    def _():
        join_image(far_turns[0])

    @pl.when(urgent_low)
    def _():
        join_image(1)

    @pl.when(urgent_high)
    def _():
        join_image(2)

    for n in range(nk):
        join_text(text_turns[n])

    @pl.when(jnp.logical_not(urgent_far))
    def _():
        join_image(far_turns[0])

    join_image(far_turns[1])

    @pl.when(jnp.logical_not(urgent_low))
    def _():
        join_image(1)

    @pl.when(jnp.logical_not(urgent_high))
    def _():
        join_image(2)

    def unit_back(unit, length, unit_grad):
        return (unit_grad - unit * jnp.sum(unit * unit_grad, axis=1, keepdims=True)) / length

    for o in range(no):
        wait(ilast.at[o], li_r.at[o])
    image_unit_grad = scale * jnp.sum(ilast[...].astype(F32), axis=0)
    image_out[...] = unit_back(image_unit, image_len, image_unit_grad)
    others = [k for k in range(nk) if k != home]
    for k in others:
        wait(tlast.at[k], lt_r.at[k])
    text_unit_grad = scale * sum((tlast[k].astype(F32) for k in others), town[home])
    text_out[...] = unit_back(text_unit, text_len, text_unit_grad)
    wait(isum, zi_s)
    wait(tbuf.at[0, 1:], zt_s)
    wait(tbuf.at[1:], pt_s)
    wait(iback, pi_s)
    wait(isend, ri_s)
    wait(tsend, rt_s)
    wait(isum, li_s)
    wait(tsum.at[1:], lt_s)


def per_device(image_emb, text_emb, labels, scale_logarithm, bias):
    rows, width = image_emb.shape
    nk, no, nq = len(TEXT_STEPS), len(IMAGE_STEPS), 2 * Y
    block = (rows, width)
    vmem = pl.BlockSpec(memory_space=pltpu.VMEM)
    hbm = pl.BlockSpec(memory_space=pltpu.HBM)
    one = pltpu.SemaphoreType.DMA
    some = lambda n: pltpu.SemaphoreType.DMA((n,))
    return pl.pallas_call(
        kernel,
        out_shape=[jax.ShapeDtypeStruct(block, F32)] * 2,
        in_specs=[hbm] * 5,
        out_specs=[vmem, vmem],
        scratch_shapes=[
            pltpu.VMEM(block, BF),
            pltpu.VMEM((X, nk) + block, BF),
            pltpu.VMEM((no, nq) + block, BF),
            pltpu.VMEM((X - 1, nk) + block, BF),
            pltpu.VMEM((no, nq - 1) + block, BF),
            pltpu.VMEM((nk,) + block, F32),
            pltpu.VMEM((no,) + block, F32),
            pltpu.VMEM((nk, X - 1) + block, BF),
            pltpu.VMEM((no, nq - 1) + block, BF),
            pltpu.VMEM((nk,) + block, BF),
            pltpu.VMEM((no,) + block, BF),
            pltpu.VMEM((nk,) + block, BF),
            pltpu.VMEM((no,) + block, BF),
            one, some(nk), one, some(no),
            one, one, one, some(no),
            one, some(nk), one, some(no),
            one, some(nk), one, some(no),
            pltpu.VMEM(block, F32),
            pltpu.VMEM(block, F32),
            pltpu.VMEM((labels.shape[0] // 128, 128), jnp.int32),
            pltpu.SMEM((1,), F32),
            pltpu.SMEM((1,), F32),
            some(5),
            pltpu.VMEM((X * nk * rows, width), F32),
            pltpu.SemaphoreType.REGULAR((2,)),
        ],
        compiler_params=pltpu.CompilerParams(
            collective_id=0, has_side_effects=True, vmem_limit_bytes=55112 * 1024
        ),
    )(labels.reshape(-1, 128), scale_logarithm, bias, image_emb, text_emb)


def solution(mesh):
    rows = P(("outer", "inner"), None)
    return jax.shard_map(
        per_device,
        mesh=mesh,
        in_specs=(rows, rows, P(), P(), P()),
        out_specs=(rows, rows),
        check_vma=False,
    )
```

```python
import functools

import jax
import jax.numpy as jnp
from jax import lax
from jax.experimental import pallas as pl
from jax.experimental.pallas import tpu as pltpu
from jax.sharding import PartitionSpec as P

EPSILON = 1e-06
X, Y, Z = 4, 4, 32
STRIDE = 4
TEXT_STEPS = (4, 3, 2, 1, 0, -1, -2, -3)
IMAGE_STEPS = (12, 4, -4, -12)
BF = jnp.bfloat16
F32 = jnp.float32


def kernel(
    labels_hbm, scale_hbm, bias_hbm, image_hbm, text_hbm,
    image_out, text_out,
    own_image, tbuf, ibuf, tsend, isend, town, iown, tback, iback,
    tsum, isum, tlast, ilast,
    zt_s, zt_r, zi_s, zi_r, pt_s, pt_r, pi_s, pi_r,
    rt_s, rt_r, ri_s, ri_r, lt_s, lt_r, li_s, li_r,
    image_ref, text_ref, labels_ref, scale_ref, bias_ref, load, tnear, ready,
):
    nk, no = len(TEXT_STEPS), len(IMAGE_STEPS)
    nq = 2 * Y
    home = TEXT_STEPS.index(0)
    rows, width = image_ref.shape
    loads = [
        pltpu.make_async_copy(src, dst, load.at[n])
        for n, (src, dst) in enumerate(
            ((image_hbm, image_ref), (text_hbm, text_ref), (labels_hbm, labels_ref),
             (scale_hbm, scale_ref), (bias_hbm, bias_ref))
        )
    ]
    for copy in loads:
        copy.start()
    x = lax.axis_index("outer")
    inner = lax.axis_index("inner")
    core = lax.rem(inner, 2)
    z = lax.rem(inner // 2, Z)
    y = inner // (2 * Z)
    side = 1 - 2 * core

    def device(dx=0, dy=0, dz=0, dc=0):
        place_y = lax.rem(y + dy + Y, Y)
        place_z = lax.rem(z + dz + Z, Z)
        place_c = lax.rem(core + dc, 2)
        return (lax.rem(x + dx + X, X), (place_y * Z + place_z) * 2 + place_c)

    def send(src, dst, send_sem, recv_sem, place):
        pltpu.make_async_remote_copy(
            src_ref=src, dst_ref=dst, send_sem=send_sem, recv_sem=recv_sem,
            device_id=place, device_id_type=pl.DeviceIdType.MESH,
        ).start()

    def wait(ref, sem):
        pltpu.make_async_copy(ref, ref, sem).wait()

    barrier = pltpu.get_barrier_semaphore()
    near = {abs(s) for s in TEXT_STEPS if s}
    partners = [device(dz=d) for a in sorted(near, reverse=True) for d in {a % Z, -a % Z}]
    partners += [device(dx=j) for j in range(1, X)]
    partners += [device(dy=q // 2, dc=q % 2) for q in range(1, nq)]
    for place in partners:
        pl.semaphore_signal(barrier, inc=1, device_id=place, device_id_type=pl.DeviceIdType.MESH)

    def normalize(values):
        length = jnp.sqrt(jnp.sum(values * values, axis=1, keepdims=True) + EPSILON)
        return values / length, length

    for copy in loads:
        copy.wait()
    image_unit, image_len = normalize(image_ref[...])
    text_unit, text_len = normalize(text_ref[...])
    own_image[...] = image_unit.astype(BF)
    tbuf[0, home] = text_unit.astype(BF)
    scale = jnp.exp(jnp.full((1, 1), scale_ref[0], F32))

    pl.semaphore_wait(barrier, len(partners))

    def spread_text(k):
        for j in range(1, X):
            send(tbuf.at[0, k], tbuf.at[j, k], pt_s, pt_r, device(dx=j))

    def spread_image(o):
        for q in range(1, nq):
            send(ibuf.at[o, 0], ibuf.at[o, q], pi_s, pi_r.at[o], device(dy=q // 2, dc=q % 2))

    for o, step in ((1, STRIDE), (2, -STRIDE)):
        send(own_image, ibuf.at[o, 0], zi_s, zi_r.at[o], device(dz=step))
        pl.semaphore_signal(
            ready.at[2 - o], inc=1, device_id=device(dz=step),
            device_id_type=pl.DeviceIdType.MESH,
        )
    for k, step in sorted(enumerate(TEXT_STEPS), key=lambda w: abs(w[1])):
        if step:
            send(tbuf.at[0, home], tbuf.at[0, k], zt_s, zt_r.at[k], device(dz=side * step))
        else:
            spread_text(home)

    urgent_low = jnp.logical_and(z >= STRIDE, z < 3 * STRIDE)
    urgent_high = jnp.logical_or(z < STRIDE, z >= Z - STRIDE)
    urgent_far = jnp.logical_and(z >= 3 * STRIDE, z < Z - STRIDE)

    lane = lax.broadcasted_iota(jnp.int32, (rows, 128), 1)
    row = lax.broadcasted_iota(jnp.int32, (rows, 128), 0)

    def label_of(step):
        pieces = []
        for q in range(nq):
            from_y = lax.rem(y - q // 2 + Y, Y)
            from_c = lax.rem(core + q % 2, 2)
            from_z = lax.rem(z - step + Z, Z)
            first = ((x * Y + from_y) * Z + from_z) * (2 * rows) + from_c * rows
            line = labels_ref[pl.ds(first // 128, 1), :]
            pick = lane == row + lax.rem(first, 128)
            pieces.append(jnp.where(pick, jnp.broadcast_to(line, (rows, 128)), 0))
        pieces = jnp.concatenate(pieces, axis=0).astype(F32)
        return jnp.sum(pieces, axis=1, keepdims=True)

    swap = lax.rem(z + IMAGE_STEPS[0], Z) < lax.rem(z - IMAGE_STEPS[0] + Z, Z)
    far_turns = [jnp.where(swap, 3, 0), jnp.where(swap, 0, 3)]
    near_label = jnp.concatenate([label_of(STRIDE), label_of(-STRIDE)], axis=0)
    far_labels = [label_of(IMAGE_STEPS[0] - 2 * STRIDE * o) for o in far_turns]

    spot = lax.broadcasted_iota(jnp.int32, (1, X * nk * rows), 1)
    at_row, at_k, at_j = spot % rows, (spot // rows) % nk, spot // (rows * nk)
    from_x = lax.rem(x - at_j + X, X)
    from_z = lax.rem(z - side * (STRIDE - at_k) + Z, Z)
    column = (((from_x * Y + y) * Z + from_z) * 2 + core) * rows + at_row
    column = column.astype(F32)

    def as_rows(block):
        return block.astype(F32).reshape(-1, width).astype(BF)

    def weigh(images, texts, label):
        similarity = lax.dot_general(
            images, texts, (((1,), (1,)), ((), ())), preferred_element_type=F32
        )
        logits = scale * similarity + bias_ref[0]
        match = label == column
        signed = jnp.where(match, -logits, logits)
        sigmoid = 1.0 / (1.0 + jnp.exp(-signed))
        return jnp.where(match, -sigmoid, sigmoid).astype(BF)

    def keep_images(grad, slots):
        grad = grad.reshape(len(slots), nq, rows, width)
        for n, o in enumerate(slots):
            iown[o] = grad[n, 0]
            isend[o] = grad[n, 1:].astype(BF)

    def return_image(o):
        for q in range(1, nq):
            send(isend.at[o, q - 1], iback.at[o, q - 1], ri_s, ri_r.at[o],
                 device(dy=-(q // 2), dc=q % 2))

    def join_image(o):
        wait(iback.at[o], ri_r.at[o])
        total = iown[o] + jnp.sum(iback[o].astype(F32), axis=0)
        isum[o] = total.astype(BF)
        send(isum.at[o], ilast.at[o], li_s, li_r.at[o],
             device(dz=2 * STRIDE * o - IMAGE_STEPS[0]))

    def pull_text(k):
        wait(tbuf.at[0, k], zt_r.at[k])
        spread_text(k)

    for k, step in sorted(enumerate(TEXT_STEPS), key=lambda w: abs(w[1])):
        if 0 < abs(step) <= STRIDE // 2:
            pull_text(k)
    start = jnp.where(urgent_high, 2, 1)
    for o in (start, 3 - start):
        step = STRIDE * (3 - 2 * o)
        wait(ibuf.at[o, 0], zi_r.at[o])
        pl.semaphore_wait(ready.at[o - 1], 1)
        far = 3 * (o - 1)
        send(ibuf.at[o, 0], ibuf.at[far, 0], zi_s, zi_r.at[far], device(dz=2 * step))
    for k, step in sorted(enumerate(TEXT_STEPS), key=lambda w: abs(w[1])):
        if abs(step) > STRIDE // 2:
            pull_text(k)
    for o in (1, 2):
        spread_image(o)

    def pull_far():
        for o in far_turns:
            wait(ibuf.at[o, 0], zi_r.at[o])
            spread_image(o)

    pull_far()

    wait(tbuf.at[1:], pt_r)
    for o in (1, 2):
        wait(ibuf.at[o, 1:], pi_r.at[o])
    texts = as_rows(tbuf[...])
    images = as_rows(ibuf[1:3])
    weights = weigh(images, texts, near_label)
    keep_images(jnp.dot(weights, texts, preferred_element_type=F32), (1, 2))
    tnear[...] = lax.dot_general(
        weights, images, (((0,), (0,)), ((), ())), preferred_element_type=F32
    )
    for n, o in enumerate(far_turns):
        wait(ibuf.at[o, 1:], pi_r.at[o])
        images = as_rows(ibuf[o])
        weights = weigh(images, texts, far_labels[n])
        keep_images(jnp.dot(weights, texts, preferred_element_type=F32), (o,))
        return_image(o)
        tnear[...] += lax.dot_general(
            weights, images, (((0,), (0,)), ((), ())), preferred_element_type=F32
        )

    low = lax.rem(z - STRIDE + core + Z, Z)
    first_text = jnp.where(low > Z - nk, Z - low, 0)
    turn = [lax.rem(first_text + n, nk) for n in range(nk)]
    text_turns = [jnp.where(core == 0, n, nk - 1 - n) for n in turn]

    grad = tnear[...].reshape(X, nk, rows, width)
    town[...] = grad[0]
    tsend[...] = grad[1:].astype(BF)
    for k in text_turns:
        for j in range(1, X):
            send(tsend.at[j - 1, k], tback.at[k, j - 1], rt_s, rt_r.at[k], device(dx=-j))

    return_image(start)
    return_image(3 - start)

    def join_text(k):
        wait(tback.at[k], rt_r.at[k])
        total = town[k] + jnp.sum(tback[k].astype(F32), axis=0)
        tsum[k] = total.astype(BF)

        @pl.when(k == home)
        def _():
            town[home] = total

        @pl.when(k != home)
        def _():
            send(tsum.at[k], tlast.at[k], lt_s, lt_r.at[k], device(dz=side * (k - STRIDE)))

    @pl.when(urgent_far)
    def _():
        join_image(far_turns[0])

    @pl.when(urgent_low)
    def _():
        join_image(1)

    @pl.when(urgent_high)
    def _():
        join_image(2)

    for n in range(nk):
        join_text(text_turns[n])

    @pl.when(jnp.logical_not(urgent_far))
    def _():
        join_image(far_turns[0])

    join_image(far_turns[1])

    @pl.when(jnp.logical_not(urgent_low))
    def _():
        join_image(1)

    @pl.when(jnp.logical_not(urgent_high))
    def _():
        join_image(2)

    def unit_back(unit, length, unit_grad):
        return (unit_grad - unit * jnp.sum(unit * unit_grad, axis=1, keepdims=True)) / length

    for o in range(no):
        wait(ilast.at[o], li_r.at[o])
    image_unit_grad = scale * jnp.sum(ilast[...].astype(F32), axis=0)
    image_out[...] = unit_back(image_unit, image_len, image_unit_grad)
    others = [k for k in range(nk) if k != home]
    for k in others:
        wait(tlast.at[k], lt_r.at[k])
    text_unit_grad = scale * sum((tlast[k].astype(F32) for k in others), town[home])
    text_out[...] = unit_back(text_unit, text_len, text_unit_grad)
    wait(isum, zi_s)
    wait(tbuf.at[0, 1:], zt_s)
    wait(tbuf.at[1:], pt_s)
    wait(iback, pi_s)
    wait(isend, ri_s)
    wait(tsend, rt_s)
    wait(isum, li_s)
    wait(tsum.at[1:], lt_s)


def per_device(image_emb, text_emb, labels, scale_logarithm, bias):
    rows, width = image_emb.shape
    nk, no, nq = len(TEXT_STEPS), len(IMAGE_STEPS), 2 * Y
    block = (rows, width)
    vmem = pl.BlockSpec(memory_space=pltpu.VMEM)
    hbm = pl.BlockSpec(memory_space=pltpu.HBM)
    one = pltpu.SemaphoreType.DMA
    some = lambda n: pltpu.SemaphoreType.DMA((n,))
    return pl.pallas_call(
        kernel,
        out_shape=[jax.ShapeDtypeStruct(block, F32)] * 2,
        in_specs=[hbm] * 5,
        out_specs=[vmem, vmem],
        scratch_shapes=[
            pltpu.VMEM(block, BF),
            pltpu.VMEM((X, nk) + block, BF),
            pltpu.VMEM((no, nq) + block, BF),
            pltpu.VMEM((X - 1, nk) + block, BF),
            pltpu.VMEM((no, nq - 1) + block, BF),
            pltpu.VMEM((nk,) + block, F32),
            pltpu.VMEM((no,) + block, F32),
            pltpu.VMEM((nk, X - 1) + block, BF),
            pltpu.VMEM((no, nq - 1) + block, BF),
            pltpu.VMEM((nk,) + block, BF),
            pltpu.VMEM((no,) + block, BF),
            pltpu.VMEM((nk,) + block, BF),
            pltpu.VMEM((no,) + block, BF),
            one, some(nk), one, some(no),
            one, one, one, some(no),
            one, some(nk), one, some(no),
            one, some(nk), one, some(no),
            pltpu.VMEM(block, F32),
            pltpu.VMEM(block, F32),
            pltpu.VMEM((labels.shape[0] // 128, 128), jnp.int32),
            pltpu.SMEM((1,), F32),
            pltpu.SMEM((1,), F32),
            some(5),
            pltpu.VMEM((X * nk * rows, width), F32),
            pltpu.SemaphoreType.REGULAR((2,)),
        ],
        compiler_params=pltpu.CompilerParams(
            collective_id=0, has_side_effects=True, vmem_limit_bytes=55112 * 1024
        ),
    )(labels.reshape(-1, 128), scale_logarithm, bias, image_emb, text_emb)


def solution(mesh):
    rows = P(("outer", "inner"), None)
    return jax.shard_map(
        per_device,
        mesh=mesh,
        in_specs=(rows, rows, P(), P(), P()),
        out_specs=(rows, rows),
        check_vma=False,
    )
```
